32 devices in a mesh: rep: 8 (over z, y), fsdp: 4 (over x, core).
Axes of the slice: x: 2, y: 2, z: 4, core: 2. Of those that a mesh axis runs over, the one named last changes fastest.
Arguments:
- tokens: bfloat16 [8192, 960], P(('rep', 'fsdp')), may hold values from -6 to 6
- cotangent: bfloat16 [8192, 960], P(('rep', 'fsdp')), may hold values from -6 to 6
- lengths: int32 [8, 8], P('rep'), may hold values from 0 to 1024, as said below
- norm1_gain: bfloat16 [960], P('fsdp'), may hold values from 0.5 to 1.5
- w_query: bfloat16 [960, 960], P('fsdp'), may hold values from -0.1875 to 0.1875
- w_key: bfloat16 [960, 320], P('fsdp'), may hold values from -0.1875 to 0.1875
- w_value: bfloat16 [960, 320], P('fsdp'), may hold values from -0.1875 to 0.1875
- w_out: bfloat16 [960, 960], P('fsdp'), may hold values from -0.75 to 0.75
- norm2_gain: bfloat16 [960], P('fsdp'), may hold values from 0.5 to 1.5
- w_gate: bfloat16 [960, 2560], P('fsdp'), may hold values from -0.1875 to 0.1875
- w_up: bfloat16 [960, 2560], P('fsdp'), may hold values from -0.1875 to 0.1875
- w_down: bfloat16 [2560, 960], P('fsdp'), may hold values from -0.125 to 0.125
Outputs:
- mixed: bfloat16 [8192, 960], P(('rep', 'fsdp'))
- tokens_grad: bfloat16 [8192, 960], P(('rep', 'fsdp'))
- norm1_grad: float32 [960], P('fsdp')
- query_grad: float32 [960, 960], P('fsdp')
- key_grad: float32 [960, 320], P('fsdp')
- value_grad: float32 [960, 320], P('fsdp')
- out_grad: float32 [960, 960], P('fsdp')
- norm2_grad: float32 [960], P('fsdp')
- gate_grad: float32 [960, 2560], P('fsdp')
- up_grad: float32 [960, 2560], P('fsdp')
- down_grad: float32 [2560, 960], P('fsdp')
The draws below stay inside these ranges and needn't reach their ends.
Inputs may be any that keep to these rules, and one draw needn't show every extreme that they name: Row g lists the lengths of the documents packed in order into the 1024 tokens of group g; each row sums to 1024; a length 0 is an empty slot.
All inputs are finite; a program needn't handle non-finite values.
Results may differ from the reference program's by a relative error of at most 0.02.
Values may be sent and summed in bfloat16 or wider, within the bound.
A program may use at most 192 MiB of HBM per device.

```python
import jax
import jax.numpy as jnp
from jax import lax

D = 960
HEADS = 15
KV_HEADS = 5
HEAD_DIM = 64
FF = 2560
TOK_DEV = 256
NSEG = 8
GROUPS = 8
GROUP_TOK = 1024
TOKENS = 8192


def draw_lengths(key, part):
    key = jax.random.fold_in(key, 11)
    first_key, second_key, third_key = jax.random.split(key, 3)
    rest = jax.random.randint(first_key, (GROUPS,), 0, TOK_DEV)
    rest = jnp.where(jnp.arange(GROUPS) == 0, 0, rest).astype(jnp.int32)
    cuts = jax.random.randint(second_key, (GROUPS, NSEG - 2), 0, rest[:, None] + 1)
    cuts = jnp.sort(cuts, axis=1)
    bounds = jnp.concatenate([jnp.zeros((GROUPS, 1), jnp.int32), cuts.astype(jnp.int32), rest[:, None]], axis=1)
    others = bounds[:, 1:] - bounds[:, :-1]
    longest = GROUP_TOK - rest
    where_long = jax.random.randint(third_key, (GROUPS, 1), 0, NSEG)
    slots = jnp.arange(NSEG)[None, :]
    source = jnp.clip(slots - (slots > where_long).astype(jnp.int32), 0, NSEG - 2)
    picked = jnp.take_along_axis(others, source, axis=1)
    return jnp.where(slots == where_long, longest[:, None], picked).astype(jnp.int32)


def block_scale(rng, extent, cuts, low, high):
    def one(dim, parts):
        draws = jax.random.uniform(jax.random.fold_in(jax.random.fold_in(rng, 6), dim), (parts,), jnp.float32, low / len(cuts), high / len(cuts))
        return jnp.repeat(jnp.exp(draws), extent[dim] // parts).reshape((-1,) + (1,) * (len(extent) - dim - 1))

    level = one(*cuts[0])
    for cut in cuts[1:]:
        level = level * one(*cut)
    return level


def bell_draw(stream_key, extent, spread, most, shards=(), kind=jnp.bfloat16):
    drawn = jax.random.normal(stream_key, extent, jnp.float32) * spread
    if len(shards) > 0:
        drawn = block_scale(stream_key, extent, shards, -0.22, 0.18) * drawn
    return jnp.clip(drawn, min=-most, max=most).astype(kind)


def setup_inputs(seed: int = 0) -> dict:
    splits = jax.random.split(jax.random.key(seed), 13)
    tokens = bell_draw(splits[0], (TOKENS, D), 1.0, 6.0, ((0, 32),))
    cotangent = bell_draw(splits[1], (TOKENS, D), 1.0, 6.0, ((0, 32),))
    lengths = draw_lengths(jax.random.fold_in(splits[12], 71), 0)
    norm1_gain = jnp.clip(1.0 + 0.1 * jax.random.normal(splits[3], (D,), jnp.float32), 0.5, 1.5).astype(jnp.bfloat16)
    w_query = bell_draw(splits[4], (D, HEADS * HEAD_DIM), D ** -0.5, 0.1875, ((0, 4),))
    w_key = bell_draw(splits[5], (D, KV_HEADS * HEAD_DIM), D ** -0.5, 0.1875, ((0, 4),))
    w_value = bell_draw(splits[6], (D, KV_HEADS * HEAD_DIM), D ** -0.5, 0.1875, ((0, 4),))
    w_out = bell_draw(splits[7], (HEADS * HEAD_DIM, D), (HEADS * HEAD_DIM // 16) ** -0.5, 0.75, ((0, 4),))
    norm2_gain = jnp.clip(1.0 + 0.1 * jax.random.normal(splits[8], (D,), jnp.float32), 0.5, 1.5).astype(jnp.bfloat16)
    w_gate = bell_draw(splits[9], (D, FF), D ** -0.5, 0.1875, ((0, 4),))
    w_up = bell_draw(splits[10], (D, FF), D ** -0.5, 0.1875, ((0, 4),))
    w_down = bell_draw(splits[11], (FF, D), FF ** -0.5, 0.125, ((0, 4),))
    return dict(tokens=tokens, cotangent=cotangent, lengths=lengths, norm1_gain=norm1_gain, w_query=w_query, w_key=w_key, w_value=w_value, w_out=w_out, norm2_gain=norm2_gain, w_gate=w_gate, w_up=w_up, w_down=w_down)


EPS = 1e-05
THETA = 100000.0

@jax.custom_vjp
def low(v):
    return lax.optimization_barrier(v.astype(jnp.bfloat16)).astype(jnp.float32)

@jax.custom_vjp
def low_back(v):
    return v

def low_keep(v):
    return (low(v), None)

def low_pass(kept, grad):
    return (grad,)

def back_keep(v):
    return (v, None)

def back_low(kept, grad):
    return (low(grad),)
low.defvjp(low_keep, low_pass)
low_back.defvjp(back_keep, back_low)

def highest(left, right):
    return jnp.dot(left, right, precision=lax.Precision.HIGHEST, preferred_element_type=jnp.float32)

def normed(values, gain):
    return values * lax.rsqrt(lax.optimization_barrier(jnp.mean(values * values, axis=-1, keepdims=True)) + EPS) * gain

def doc_layout(lens, count):
    ends = jnp.cumsum(lens).astype(jnp.int32)
    starts = (ends - lens).astype(jnp.int32)
    place = jnp.arange(count, dtype=jnp.int32)
    segment = lax.optimization_barrier(jnp.sum((place[:, None] >= ends[None, :]).astype(jnp.int32), axis=1)).astype(jnp.int32)
    owner = segment[:, None] == jnp.arange(lens.shape[0], dtype=jnp.int32)[None, :]
    offset = lax.optimization_barrier(jnp.sum(jnp.where(owner, starts[None, :], 0), axis=1)).astype(jnp.int32)
    return (segment, (place - offset).astype(jnp.int32))

def rotate(heads, position, sign):
    half = heads.shape[-1] // 2
    freq = THETA ** (-jnp.arange(half, dtype=jnp.float32) * 2.0 / heads.shape[-1])
    angle = position.astype(jnp.float32)[:, None] * freq[None, :]
    cosine = jnp.cos(angle)[:, None, :]
    sine = sign * jnp.sin(angle)[:, None, :]
    first = heads[..., :half]
    second = heads[..., half:]
    return jnp.concatenate([first * cosine - second * sine, second * cosine + first * sine], axis=-1)

def attend(query, keys, values, segment):
    count = query.shape[0]
    block = min(512, count)
    groups = keys.shape[1]
    share = query.shape[1] // groups
    scale = HEAD_DIM ** (-0.5)
    grouped = query.reshape(count // block, block, groups, share, HEAD_DIM)
    key_place = jnp.arange(count, dtype=jnp.int32)

    @jax.checkpoint
    def one_block(item):
        piece, start = item
        place = start + jnp.arange(block, dtype=jnp.int32)
        mine = lax.dynamic_slice_in_dim(segment, start, block)
        raw = jnp.einsum('bgrd,kgd->grbk', piece, keys, precision=lax.Precision.HIGHEST) * scale
        raw = low_back(raw)
        allowed = (key_place[None, :] <= place[:, None]) & (segment[None, :] == mine[:, None])
        masked = jnp.where(allowed, raw, -1e+30)
        top = lax.optimization_barrier(jnp.max(masked, axis=-1, keepdims=True))
        expo = jnp.exp(masked - top)
        probs = expo / lax.optimization_barrier(jnp.sum(expo, axis=-1, keepdims=True))
        result = jnp.einsum('grbk,kgd->bgrd', low(probs), values, precision=lax.Precision.HIGHEST)
        return result.reshape(block, -1)
    starts = jnp.arange(count // block, dtype=jnp.int32) * block
    return lax.map(one_block, (grouped, starts)).reshape(count, -1)

def layer(inputs, weights, segment, position):
    gain_one, w_query, w_key, w_value, w_out, gain_two, w_gate, w_up, w_down = weights
    count = inputs.shape[0]
    normed_one = low(normed(inputs, gain_one))
    query = rotate(low_back(highest(normed_one, w_query)).reshape(count, -1, HEAD_DIM), position, 1.0)
    keys = rotate(low_back(highest(normed_one, w_key)).reshape(count, -1, HEAD_DIM), position, 1.0)
    query = low(query)
    keys = low(keys)
    values = low(low_back(highest(normed_one, w_value))).reshape(count, -1, HEAD_DIM)
    attended = attend(query, keys, values, segment)
    branch = low_back(highest(low(low_back(attended)), w_out))
    resid = inputs + branch
    normed_two = low(normed(resid, gain_two))
    gate = low_back(highest(normed_two, w_gate))
    up_proj = low_back(highest(normed_two, w_up))
    hidden = low(jax.nn.silu(gate) * up_proj)
    return resid + highest(hidden, w_down)

def reference(tokens, cotangent, lengths, norm1_gain, w_query, w_key, w_value, w_out, norm2_gain, w_gate, w_up, w_down):
    params = tuple((weight.astype(jnp.float32) for weight in (norm1_gain, w_query, w_key, w_value, w_out, norm2_gain, w_gate, w_up, w_down)))
    inputs = tokens.astype(jnp.float32).reshape(GROUPS, GROUP_TOK, D)
    grads_in = cotangent.astype(jnp.float32).reshape(GROUPS, GROUP_TOK, D)

    def one_group(totals, item):
        block_in, block_grad, lens = item
        segment, position = doc_layout(lens, GROUP_TOK)

        def forward(values, weights):
            return layer(values, weights, segment, position)
        result, pull = jax.vjp(forward, block_in, params)
        grad_in, grad_weights = pull(block_grad)
        return (jax.tree.map(jnp.add, totals, grad_weights), (result, grad_in))
    zeros = jax.tree.map(jnp.zeros_like, params)
    totals, outputs = lax.scan(one_group, zeros, (inputs, grads_in, lengths))
    results, grad_inputs = outputs
    return (results.reshape(TOKENS, D).astype(jnp.bfloat16), grad_inputs.reshape(TOKENS, D).astype(jnp.bfloat16), totals[0], totals[1], totals[2], totals[3], totals[4], totals[5], totals[6], totals[7], totals[8])
```

```python
import functools

import jax
import jax.numpy as jnp
from jax import lax
from jax.experimental import pallas as pl
from jax.experimental.pallas import tpu as pltpu
from jax.sharding import PartitionSpec as P

HEAD_DIM = 64


EPS = 1e-05
THETA = 100000.0


def doc_layout(lens, count):
    ends = jnp.cumsum(lens)
    starts = ends - lens
    place = jnp.arange(count, dtype=jnp.int32)
    segment = jnp.sum((place[:, None] >= ends[None, :]).astype(jnp.int32), axis=1)
    owner = segment[:, None] == jnp.arange(lens.shape[0], dtype=jnp.int32)[None, :]
    offset = jnp.sum(jnp.where(owner, starts[None, :], 0), axis=1)
    return (segment, place - offset)


def rotate(heads, position, sign):
    half = heads.shape[-1] // 2
    freq = THETA ** (-jnp.arange(half, dtype=jnp.float32) * 2.0 / heads.shape[-1])
    angle = position.astype(jnp.float32)[:, None] * freq[None, :]
    cosine = jnp.cos(angle)[:, None, :]
    sine = sign * jnp.sin(angle)[:, None, :]
    first = heads[..., :half]
    second = heads[..., half:]
    return jnp.concatenate(
        [first * cosine - second * sine, second * cosine + first * sine], axis=-1
    )


def matmul(left, right):
    return jnp.dot(left, right, preferred_element_type=jnp.float32)


def left_inner(left, right):
    return lax.dot_general(
        left, right, (((0,), (0,)), ((), ())), preferred_element_type=jnp.float32
    )


def right_inner(left, right):
    return lax.dot_general(
        left, right, (((1,), (1,)), ((), ())), preferred_element_type=jnp.float32
    )


def norm_back(values, inverse, gain, upstream):
    scaled = gain * upstream
    gain_part = jnp.sum(upstream * values * inverse, axis=0)
    input_part = inverse * scaled - values * inverse**3 * jnp.mean(
        scaled * values, axis=-1, keepdims=True
    )
    return (gain_part, input_part)


MESH = pl.DeviceIdType.MESH


def cut(extent, unit, most):
    pieces = []
    start = 0
    while start < extent:
        size = unit
        while size * 2 <= min(most, extent - start):
            size *= 2
        pieces.append((start, size))
        start += size
    return pieces


def row_block(rows):
    for block in (80, 64, 48, 32, 16):
        if rows % block == 0:
            return block
    return rows


class Chunk:
    def __init__(self, source, dim, rows, columns, owner_rows, bits):
        self.source = source
        self.dim = dim
        self.rows = rows
        self.columns = columns
        self.owner_rows = owner_rows
        unit = 128 if dim == 1 else 16
        size = (rows[1], columns[1])[dim]
        self.sizes = [size]
        self.halved = []
        for _ in range(bits):
            half = size % (2 * unit) == 0
            self.halved.append(half)
            size = size // 2 if half else size
            self.sizes.append(size)

    def shape(self, level):
        full = [self.rows[1], self.columns[1]]
        full[self.dim] = self.sizes[level]
        return tuple(full)


def span(ref, dim, start, size):
    unit = 128 if dim == 1 else 16
    part = pl.ds(pl.multiple_of(start, unit), size)
    return ref.at[:, part] if dim == 1 else ref.at[part, :]


def add_into(target, other):
    rows = target.shape[0]
    block = row_block(rows)

    def step(i, carry):
        part = pl.ds(pl.multiple_of(i * block, 16), block)
        total = target[part, :].astype(jnp.float32) + other[part, :].astype(jnp.float32)
        target[part, :] = total.astype(target.dtype)
        return carry

    lax.fori_loop(0, rows // block, step, 0)


def reduce_kernel(chunks, bits, *refs):
    sources, gains = refs[:3], refs[3]
    outs, gain_out = refs[4:7], refs[7]
    scratch = list(refs[8:])
    buffers = []
    for chunk in chunks:
        count = 4 + bits
        buffers.append(scratch[:count])
        scratch = scratch[count:]
    gain_sum, gain_got, send_sem, recv_sem, local_sem, gain_send, gain_recv, out_sem = scratch
    rep, fsdp = lax.axis_index("rep"), lax.axis_index("fsdp")
    core, far = lax.rem(fsdp, 2), lax.div(fsdp, 2)
    digits = [lax.rem(lax.div(rep, 2**k), 2) for k in range(bits)]
    sibling = (rep, far * 2 + 1 - core)
    across = (rep, (1 - far) * 2 + core)
    peers = [(rep + (1 - 2 * digits[k]) * 2**k, fsdp) for k in range(bits)]
    stages = [sibling, across] + peers

    barrier = pltpu.get_barrier_semaphore()
    for peer in stages:
        pl.semaphore_signal(barrier, inc=1, device_id=peer, device_id_type=MESH)
    pl.semaphore_wait(barrier, len(stages))

    waiting = []
    per_chunk = 3 + 2 * bits

    def send(c, slot, src, dst, peer):
        place = c * per_chunk + slot
        copy = pltpu.make_async_remote_copy(
            src_ref=src,
            dst_ref=dst,
            send_sem=send_sem.at[place],
            recv_sem=recv_sem.at[place],
            device_id=peer,
            device_id_type=MESH,
        )
        copy.start()
        waiting.append(copy)
        return copy

    def run_chunk(c, chunk):
        own, near = buffers[c][0], buffers[c][1]
        levels = buffers[c][2 : 3 + bits]
        result = buffers[c][3 + bits]
        source = sources[chunk.source]
        columns = pl.ds(*chunk.columns)

        def block(owner):
            start = pl.multiple_of(owner * chunk.owner_rows + chunk.rows[0], 16)
            return source.at[pl.ds(start, chunk.rows[1]), columns]

        copies = [send(c, i, block(2 * i + 1 - core), near.at[i], sibling) for i in range(2)]
        locals_ = []
        for i in range(2):
            copy = pltpu.make_async_copy(
                block(2 * i + core), own.at[i], local_sem.at[2 * c + i]
            )
            copy.start()
            locals_.append(copy)
        yield
        for copy in copies:
            copy.wait_recv()
        for copy in locals_:
            copy.wait()
        for i in range(2):
            add_into(near.at[i], own.at[i])
        copy = send(c, 2, near.at[1 - far], levels[0], across)
        yield
        copy.wait_recv()
        add_into(levels[0], near.at[far])
        offset = 0
        offsets = []
        for k in range(bits):
            size = chunk.sizes[k + 1]
            if chunk.halved[k]:
                src = span(levels[k], chunk.dim, (1 - digits[k]) * size, size)
                keep = span(levels[k], chunk.dim, digits[k] * size, size)
                offset = offset + digits[k] * size
            else:
                src = keep = levels[k]
            offsets.append(offset)
            copy = send(c, 3 + k, src, levels[k + 1], peers[k])
            yield
            copy.wait_recv()
            add_into(levels[k + 1], keep)
        mine = span(result, chunk.dim, offset, chunk.sizes[bits])
        mine[...] = levels[bits][...]
        for k in reversed(range(bits)):
            if not chunk.halved[k]:
                continue
            part = span(result, chunk.dim, offsets[k], chunk.sizes[k + 1])
            copy = send(c, 3 + bits + k, part, part, peers[k])
            yield
            copy.wait_recv()
        rows = pl.ds(*chunk.rows)
        copy = pltpu.make_async_copy(
            result, outs[chunk.source].at[rows, columns], out_sem.at[c]
        )
        copy.start()
        locals_.append(copy)
        final.append(copy)

    final = []

    def run_gains():
        gain_sum[0] = gains[...]
        for s, peer in enumerate(stages):
            copy = pltpu.make_async_remote_copy(
                src_ref=gain_sum.at[s],
                dst_ref=gain_got.at[s],
                send_sem=gain_send.at[s],
                recv_sem=gain_recv.at[s],
                device_id=peer,
                device_id_type=MESH,
            )
            copy.start()
            waiting.append(copy)
            yield
            copy.wait_recv()
            gain_sum[s + 1] = gain_sum[s] + gain_got[s]
        gain_out[...] = gain_sum[len(stages)]

    todo = [run_chunk(c, chunk) for c, chunk in enumerate(chunks)] + [run_gains()]
    active = []
    while todo or active:
        if todo:
            active.insert(0, todo.pop(0))
        left = []
        for task in active:
            try:
                next(task)
                left.append(task)
            except StopIteration:
                pass
        active = left
    for copy in waiting:
        copy.wait_send()
    for copy in final:
        copy.wait()


def reduce_grads(attn, ffn, down, gains):
    ways = lax.axis_size("fsdp")
    bits = lax.axis_size("rep").bit_length() - 1
    chunks = []
    for source, array in ((1, ffn), (0, attn)):
        rows = array.shape[0] // ways
        for part in cut(array.shape[1], 512, 2048):
            chunks.append(Chunk(source, 1, (0, rows), part, rows, bits))
    rows = down.shape[0] // ways
    first = (rows * 3 // 5) // 16 * 16
    for part in ((0, first), (first, rows - first)):
        chunks.append(Chunk(2, 0, part, (0, down.shape[1]), rows, bits))
    low = jnp.bfloat16
    scratch = []
    for chunk in chunks:
        full = chunk.shape(0)
        scratch += [pltpu.VMEM((2,) + full, low)] * 2
        scratch += [pltpu.VMEM(chunk.shape(k), low) for k in range(bits + 1)]
        scratch.append(pltpu.VMEM(full, low))
    stages = bits + 2
    per_chunk = 3 + 2 * bits
    scratch += [
        pltpu.VMEM((stages + 1,) + gains.shape, jnp.float32),
        pltpu.VMEM((stages,) + gains.shape, jnp.float32),
        pltpu.SemaphoreType.DMA((len(chunks) * per_chunk,)),
        pltpu.SemaphoreType.DMA((len(chunks) * per_chunk,)),
        pltpu.SemaphoreType.DMA((len(chunks) * 2,)),
        pltpu.SemaphoreType.DMA((stages,)),
        pltpu.SemaphoreType.DMA((stages,)),
        pltpu.SemaphoreType.DMA((len(chunks),)),
    ]
    anywhere = pl.BlockSpec(memory_space=pl.ANY)
    in_vmem = pl.BlockSpec(memory_space=pltpu.VMEM)
    return pl.pallas_call(
        functools.partial(reduce_kernel, chunks, bits),
        out_shape=tuple(
            jax.ShapeDtypeStruct((a.shape[0] // ways, a.shape[1]), low) for a in (attn, ffn, down)
        )
        + (jax.ShapeDtypeStruct(gains.shape, jnp.float32),),
        in_specs=[anywhere] * 3 + [in_vmem],
        out_specs=(anywhere,) * 3 + (in_vmem,),
        scratch_shapes=scratch,
        compiler_params=pltpu.CompilerParams(
            collective_id=0, has_side_effects=True, vmem_limit_bytes=56 * 2**20
        ),
        name="reduce_grads",
    )(attn, ffn, down, gains)


def body(
    tokens,
    cotangent,
    lengths,
    norm1_gain,
    w_query,
    w_key,
    w_value,
    w_out,
    norm2_gain,
    w_gate,
    w_up,
    w_down,
):
    gathered = (
        lax.all_gather(norm1_gain, "fsdp", axis=0, tiled=True),
        lax.all_gather(w_query, "fsdp", axis=0, tiled=True),
        lax.all_gather(w_key, "fsdp", axis=0, tiled=True),
        lax.all_gather(w_value, "fsdp", axis=0, tiled=True),
        lax.all_gather(w_out, "fsdp", axis=0, tiled=True),
        lax.all_gather(norm2_gain, "fsdp", axis=0, tiled=True),
        lax.all_gather(w_gate, "fsdp", axis=0, tiled=True),
        lax.all_gather(w_up, "fsdp", axis=0, tiled=True),
        lax.all_gather(w_down, "fsdp", axis=0, tiled=True),
    )
    (
        gain_one,
        query_weight,
        key_weight,
        value_weight,
        out_weight,
        gain_two,
        gate_weight,
        up_weight,
        down_weight,
    ) = gathered
    count = tokens.shape[0]
    ways = lax.axis_size("fsdp")
    total = count * ways
    head_dim = HEAD_DIM
    scale = head_dim ** (-0.5)
    segment_all, position_all = doc_layout(lengths[0], total)
    first_row = lax.axis_index("fsdp") * count
    segment_mine = lax.dynamic_slice_in_dim(segment_all, first_row, count)
    position_mine = lax.dynamic_slice_in_dim(position_all, first_row, count)
    place_mine = first_row + jnp.arange(count, dtype=jnp.int32)
    inputs = tokens.astype(jnp.float32)
    inverse_one = lax.rsqrt(jnp.mean(inputs * inputs, axis=-1, keepdims=True) + EPS)
    gain_one_f = gain_one.astype(jnp.float32)
    normed_one = (inputs * inverse_one * gain_one_f).astype(jnp.bfloat16)
    query = rotate(
        matmul(normed_one, query_weight).reshape(count, -1, head_dim), position_mine, 1.0
    ).astype(jnp.bfloat16)
    key_local = rotate(
        matmul(normed_one, key_weight).reshape(count, -1, head_dim), position_mine, 1.0
    ).astype(jnp.bfloat16)
    value_local = matmul(normed_one, value_weight).astype(jnp.bfloat16)
    all_keys, all_values = (
        lax.all_gather(key_local.reshape(count, -1), "fsdp", axis=0, tiled=True),
        lax.all_gather(value_local, "fsdp", axis=0, tiled=True),
    )
    groups = all_keys.shape[1] // head_dim
    share = query.shape[1] // groups
    grouped = query.reshape(count, groups, share, head_dim)
    key_block = min(512, total)
    nblocks = total // key_block
    key_blocks = all_keys.reshape(nblocks, key_block, groups, head_dim)
    value_blocks = all_values.reshape(nblocks, key_block, groups, head_dim)
    segment_blocks = segment_all.reshape(nblocks, key_block)
    place_blocks = jnp.arange(total, dtype=jnp.int32).reshape(nblocks, key_block)

    def scores_for(keys_here, segment_here, place_here):
        allowed = (place_here[None, :] <= place_mine[:, None]) & (
            segment_here[None, :] == segment_mine[:, None]
        )
        raw = (
            jnp.einsum("bgrd,kgd->grbk", grouped, keys_here, preferred_element_type=jnp.float32)
            * scale
        )
        return (jnp.where(allowed[None, None], raw, -1e30), allowed[None, None])

    def gather_stats(carry, item):
        top, mass = carry
        keys_here, values_here, segment_here, place_here = item
        raw, allowed = scores_for(keys_here, segment_here, place_here)
        new_top = jnp.maximum(top, jnp.max(raw, axis=-1, keepdims=True))
        expo = jnp.where(allowed, jnp.exp(raw - new_top), 0.0)
        mass = mass * jnp.exp(top - new_top) + jnp.sum(expo, axis=-1, keepdims=True)
        return ((new_top, mass), None)

    stack = (key_blocks, value_blocks, segment_blocks, place_blocks)
    start_top = jnp.full((groups, share, count, 1), -1e30, jnp.float32)
    start_mass = jnp.zeros((groups, share, count, 1), jnp.float32)
    (top_all, mass_all), unused = lax.scan(gather_stats, (start_top, start_mass), stack)
    log_total = top_all + jnp.log(mass_all)

    def probs_for(item):
        keys_here, values_here, segment_here, place_here = item
        raw, allowed = scores_for(keys_here, segment_here, place_here)
        return jnp.where(allowed, jnp.exp(raw - log_total), 0.0)

    def mix_values(carry, item):
        probs = probs_for(item).astype(jnp.bfloat16)
        return (
            carry
            + jnp.einsum("grbk,kgd->bgrd", probs, item[1], preferred_element_type=jnp.float32),
            None,
        )

    attended, unused = lax.scan(
        mix_values, jnp.zeros((count, groups, share, head_dim), jnp.float32), stack
    )
    attended_flat = attended.reshape(count, -1)
    attended_low = attended_flat.astype(jnp.bfloat16)
    resid = inputs + matmul(attended_low, out_weight)
    inverse_two = lax.rsqrt(jnp.mean(resid * resid, axis=-1, keepdims=True) + EPS)
    gain_two_f = gain_two.astype(jnp.float32)
    normed_two = (resid * inverse_two * gain_two_f).astype(jnp.bfloat16)
    gate = matmul(normed_two, gate_weight)
    up_proj = matmul(normed_two, up_weight)
    sigma = jax.nn.sigmoid(gate)
    activated = gate * sigma
    hidden = (activated * up_proj).astype(jnp.bfloat16)
    mixed = (resid + matmul(hidden, down_weight)).astype(jnp.bfloat16)
    upstream = cotangent.astype(jnp.float32)
    down_grad = left_inner(hidden, cotangent)
    hidden_back = right_inner(cotangent, down_weight)
    gate_back = (hidden_back * up_proj * sigma * (1.0 + gate * (1.0 - sigma))).astype(jnp.bfloat16)
    up_back = (hidden_back * activated).astype(jnp.bfloat16)
    ffn_grad = left_inner(normed_two, jnp.concatenate([gate_back, up_back], axis=1))
    normed_two_back = right_inner(gate_back, gate_weight) + right_inner(up_back, up_weight)
    norm2_grad, resid_part = norm_back(resid, inverse_two, gain_two_f, normed_two_back)
    resid_back = upstream + resid_part
    branch_back = resid_back.astype(jnp.bfloat16)
    out_grad = left_inner(attended_low, branch_back)
    attended_back = right_inner(branch_back, out_weight).astype(jnp.bfloat16)
    back_heads = attended_back.reshape(count, groups, share, head_dim)
    delta = jnp.sum(back_heads.astype(jnp.float32) * attended, axis=-1).transpose(1, 2, 0)[
        ..., None
    ]

    def attend_back(carry, item):
        probs = probs_for(item)
        keys_here = item[0]
        values_here = item[1]
        values_back = jnp.einsum(
            "grbk,bgrd->kgd",
            probs.astype(jnp.bfloat16),
            back_heads,
            preferred_element_type=jnp.float32,
        )
        prob_back = jnp.einsum(
            "bgrd,kgd->grbk", back_heads, values_here, preferred_element_type=jnp.float32
        )
        score_back = (probs * (prob_back - delta)).astype(jnp.bfloat16)
        carry = carry + jnp.einsum(
            "grbk,kgd->bgrd", score_back, keys_here, preferred_element_type=jnp.float32
        )
        keys_back = (
            jnp.einsum("grbk,bgrd->kgd", score_back, grouped, preferred_element_type=jnp.float32)
            * scale
        )
        return (carry, (keys_back, values_back))

    query_acc, kv_back = lax.scan(
        attend_back, jnp.zeros((count, groups, share, head_dim), jnp.float32), stack
    )
    keys_back_all = kv_back[0].reshape(total, -1)
    values_back_all = kv_back[1].reshape(total, -1)
    keys_back, values_back = (
        lax.psum_scatter(
            keys_back_all.astype(jnp.bfloat16), "fsdp", scatter_dimension=0, tiled=True
        ).astype(jnp.float32),
        lax.psum_scatter(
            values_back_all.astype(jnp.bfloat16), "fsdp", scatter_dimension=0, tiled=True
        ).astype(jnp.float32),
    )
    key_pre = (
        rotate(keys_back.reshape(count, -1, head_dim), position_mine, -1.0)
        .reshape(count, -1)
        .astype(jnp.bfloat16)
    )
    value_pre = values_back.astype(jnp.bfloat16)
    query_pre = (
        rotate((query_acc * scale).reshape(count, -1, head_dim), position_mine, -1.0)
        .reshape(count, -1)
        .astype(jnp.bfloat16)
    )
    qkv_grad = left_inner(normed_one, jnp.concatenate([query_pre, key_pre, value_pre], axis=1))
    normed_one_back = (
        right_inner(query_pre, query_weight)
        + right_inner(key_pre, key_weight)
        + right_inner(value_pre, value_weight)
    )
    norm1_grad, input_part = norm_back(inputs, inverse_one, gain_one_f, normed_one_back)
    tokens_grad = (resid_back + input_part).astype(jnp.bfloat16)
    low = jnp.bfloat16
    attn_grad = jnp.concatenate([qkv_grad.astype(low), out_grad.astype(low)], axis=1)
    gains = jnp.stack([norm1_grad, norm2_grad])
    gains = jnp.pad(gains, ((0, 6), (0, -gains.shape[1] % 128)))
    attn_sum, ffn_sum, down_sum, gain_sum = reduce_grads(
        attn_grad, ffn_grad.astype(low), down_grad.astype(low), gains
    )
    mine = lax.axis_index("fsdp") * norm1_gain.shape[0]
    gain_rows = lax.dynamic_slice_in_dim(gain_sum, mine, norm1_gain.shape[0], axis=1)
    results = []
    offset = 0
    for shard in (w_query, w_key, w_value, w_out):
        results.append(attn_sum[:, offset : offset + shard.shape[1]].astype(jnp.float32))
        offset += shard.shape[1]
    hidden_size = w_gate.shape[1]
    return (
        mixed,
        tokens_grad,
        gain_rows[0],
        results[0],
        results[1],
        results[2],
        results[3],
        gain_rows[1],
        ffn_sum[:, :hidden_size].astype(jnp.float32),
        ffn_sum[:, hidden_size:].astype(jnp.float32),
        down_sum.astype(jnp.float32),
    )


def solution(mesh):
    return jax.shard_map(
        body,
        mesh=mesh,
        in_specs=(
            P(("rep", "fsdp"), None),
            P(("rep", "fsdp"), None),
            P("rep", None),
            P("fsdp"),
            P("fsdp", None),
            P("fsdp", None),
            P("fsdp", None),
            P("fsdp", None),
            P("fsdp"),
            P("fsdp", None),
            P("fsdp", None),
            P("fsdp", None),
        ),
        out_specs=(
            P(("rep", "fsdp"), None),
            P(("rep", "fsdp"), None),
            P("fsdp"),
            P("fsdp", None),
            P("fsdp", None),
            P("fsdp", None),
            P("fsdp", None),
            P("fsdp"),
            P("fsdp", None),
            P("fsdp", None),
            P("fsdp", None),
        ),
        check_vma=False,
    )
```

```python
import functools

import jax
import jax.numpy as jnp
from jax import lax
from jax.experimental import pallas as pl
from jax.experimental.pallas import tpu as pltpu
from jax.sharding import PartitionSpec as P

HEAD_DIM = 64


EPS = 1e-05
THETA = 100000.0


def doc_layout(lens, count):
    ends = jnp.cumsum(lens)
    starts = ends - lens
    place = jnp.arange(count, dtype=jnp.int32)
    segment = jnp.sum((place[:, None] >= ends[None, :]).astype(jnp.int32), axis=1)
    owner = segment[:, None] == jnp.arange(lens.shape[0], dtype=jnp.int32)[None, :]
    offset = jnp.sum(jnp.where(owner, starts[None, :], 0), axis=1)
    return (segment, place - offset)


def rotate(heads, position, sign):
    half = heads.shape[-1] // 2
    freq = THETA ** (-jnp.arange(half, dtype=jnp.float32) * 2.0 / heads.shape[-1])
    angle = position.astype(jnp.float32)[:, None] * freq[None, :]
    cosine = jnp.cos(angle)[:, None, :]
    sine = sign * jnp.sin(angle)[:, None, :]
    first = heads[..., :half]
    second = heads[..., half:]
    return jnp.concatenate(
        [first * cosine - second * sine, second * cosine + first * sine], axis=-1
    )


def matmul(left, right):
    return jnp.dot(left, right, preferred_element_type=jnp.float32)


def left_inner(left, right):
    return lax.dot_general(
        left, right, (((0,), (0,)), ((), ())), preferred_element_type=jnp.float32
    )


def right_inner(left, right):
    return lax.dot_general(
        left, right, (((1,), (1,)), ((), ())), preferred_element_type=jnp.float32
    )


def norm_back(values, inverse, gain, upstream):
    scaled = gain * upstream
    gain_part = jnp.sum(upstream * values * inverse, axis=0)
    input_part = inverse * scaled - values * inverse**3 * jnp.mean(
        scaled * values, axis=-1, keepdims=True
    )
    return (gain_part, input_part)


MESH = pl.DeviceIdType.MESH


MOST = 512
GATHER_MOST = 1024
REDUCE_AHEAD = 1
GATHER_AHEAD = 1


def run_staggered(todo, ahead):
    active = []
    early = []
    while todo or early or active:
        while todo and len(early) < ahead:
            early.append(todo.pop(0))
            next(early[-1])
        if early:
            active.insert(0, early.pop(0))
        if todo:
            early.append(todo.pop(0))
            next(early[-1])
        left = []
        for task in active:
            try:
                next(task)
                left.append(task)
            except StopIteration:
                pass
        active = left


def cut(extent, unit, most):
    pieces = []
    start = 0
    while start < extent:
        size = unit
        while size * 2 <= min(most, extent - start):
            size *= 2
        pieces.append((start, size))
        start += size
    return pieces


def row_block(rows):
    for block in (80, 64, 48, 32, 16):
        if rows % block == 0:
            return block
    return rows


class Chunk:
    def __init__(self, source, dim, rows, columns, owner_rows, bits):
        self.source = source
        self.dim = dim
        self.rows = rows
        self.columns = columns
        self.owner_rows = owner_rows
        unit = 128 if dim == 1 else 16
        size = (rows[1], columns[1])[dim]
        self.sizes = [size]
        self.halved = []
        for _ in range(bits):
            half = size % (2 * unit) == 0
            self.halved.append(half)
            size = size // 2 if half else size
            self.sizes.append(size)

    def shape(self, level):
        full = [self.rows[1], self.columns[1]]
        full[self.dim] = self.sizes[level]
        return tuple(full)


def span(ref, dim, start, size):
    unit = 128 if dim == 1 else 16
    part = pl.ds(pl.multiple_of(start, unit), size)
    return ref.at[:, part] if dim == 1 else ref.at[part, :]


def add_into(target, other):
    rows = target.shape[0]
    block = row_block(rows)

    def step(i, carry):
        part = pl.ds(pl.multiple_of(i * block, 16), block)
        total = target[part, :].astype(jnp.float32) + other[part, :].astype(jnp.float32)
        target[part, :] = total.astype(target.dtype)
        return carry

    lax.fori_loop(0, rows // block, step, 0)


def reduce_kernel(chunks, bits, *refs):
    sources, gains = refs[:3], refs[3]
    outs, gain_out = refs[4:7], refs[7]
    scratch = list(refs[8:])
    buffers = []
    for chunk in chunks:
        count = 4 + bits
        buffers.append(scratch[:count])
        scratch = scratch[count:]
    gain_sum, gain_got, send_sem, recv_sem, local_sem, gain_send, gain_recv, out_sem = scratch
    rep, fsdp = lax.axis_index("rep"), lax.axis_index("fsdp")
    core, far = lax.rem(fsdp, 2), lax.div(fsdp, 2)
    digits = [lax.rem(lax.div(rep, 2**k), 2) for k in range(bits)]
    sibling = (rep, far * 2 + 1 - core)
    across = (rep, (1 - far) * 2 + core)
    peers = [(rep + (1 - 2 * digits[k]) * 2**k, fsdp) for k in range(bits)]
    stages = [sibling, across] + peers

    barrier = pltpu.get_barrier_semaphore()
    for peer in stages:
        pl.semaphore_signal(barrier, inc=1, device_id=peer, device_id_type=MESH)
    pl.semaphore_wait(barrier, len(stages))

    waiting = []
    per_chunk = 3 + 2 * bits

    def send(c, slot, src, dst, peer):
        place = c * per_chunk + slot
        copy = pltpu.make_async_remote_copy(
            src_ref=src,
            dst_ref=dst,
            send_sem=send_sem.at[place],
            recv_sem=recv_sem.at[place],
            device_id=peer,
            device_id_type=MESH,
        )
        copy.start()
        waiting.append(copy)
        return copy

    def run_chunk(c, chunk):
        own, near = buffers[c][0], buffers[c][1]
        levels = buffers[c][2 : 3 + bits]
        result = buffers[c][3 + bits]
        source = sources[chunk.source]
        columns = pl.ds(*chunk.columns)

        def block(owner):
            start = pl.multiple_of(owner * chunk.owner_rows + chunk.rows[0], 16)
            return source.at[pl.ds(start, chunk.rows[1]), columns]

        copies = [send(c, i, block(2 * i + 1 - core), near.at[i], sibling) for i in range(2)]
        locals_ = []
        for i in range(2):
            copy = pltpu.make_async_copy(
                block(2 * i + core), own.at[i], local_sem.at[2 * c + i]
            )
            copy.start()
            locals_.append(copy)
        yield
        for copy in copies:
            copy.wait_recv()
        for copy in locals_:
            copy.wait()
        for i in range(2):
            add_into(near.at[i], own.at[i])
        copy = send(c, 2, near.at[1 - far], levels[0], across)
        yield
        copy.wait_recv()
        add_into(levels[0], near.at[far])
        offset = 0
        offsets = []
        for k in range(bits):
            size = chunk.sizes[k + 1]
            if chunk.halved[k]:
                src = span(levels[k], chunk.dim, (1 - digits[k]) * size, size)
                keep = span(levels[k], chunk.dim, digits[k] * size, size)
                offset = offset + digits[k] * size
            else:
                src = keep = levels[k]
            offsets.append(offset)
            copy = send(c, 3 + k, src, levels[k + 1], peers[k])
            yield
            copy.wait_recv()
            add_into(levels[k + 1], keep)
        mine = span(result, chunk.dim, offset, chunk.sizes[bits])
        mine[...] = levels[bits][...]
        for k in reversed(range(bits)):
            if not chunk.halved[k]:
                continue
            part = span(result, chunk.dim, offsets[k], chunk.sizes[k + 1])
            copy = send(c, 3 + bits + k, part, part, peers[k])
            yield
            copy.wait_recv()
        rows = pl.ds(*chunk.rows)
        copy = pltpu.make_async_copy(
            result, outs[chunk.source].at[rows, columns], out_sem.at[c]
        )
        copy.start()
        locals_.append(copy)
        final.append(copy)

    final = []

    def run_gains():
        gain_sum[0] = gains[...]
        for s, peer in enumerate(stages):
            copy = pltpu.make_async_remote_copy(
                src_ref=gain_sum.at[s],
                dst_ref=gain_got.at[s],
                send_sem=gain_send.at[s],
                recv_sem=gain_recv.at[s],
                device_id=peer,
                device_id_type=MESH,
            )
            copy.start()
            waiting.append(copy)
            yield
            copy.wait_recv()
            gain_sum[s + 1] = gain_sum[s] + gain_got[s]
        gain_out[...] = gain_sum[len(stages)]

    todo = [run_chunk(c, chunk) for c, chunk in enumerate(chunks)] + [run_gains()]
    run_staggered(todo, REDUCE_AHEAD)
    for copy in waiting:
        copy.wait_send()
    for copy in final:
        copy.wait()


def reduce_grads(attn, ffn, down, gains):
    ways = lax.axis_size("fsdp")
    bits = lax.axis_size("rep").bit_length() - 1
    chunks = []
    for source, array in ((1, ffn), (0, attn)):
        rows = array.shape[0] // ways
        for part in cut(array.shape[1], 512, MOST):
            chunks.append(Chunk(source, 1, (0, rows), part, rows, bits))
    rows = down.shape[0] // ways
    for part in cut(rows, 128, 256):
        chunks.append(Chunk(2, 0, part, (0, down.shape[1]), rows, bits))
    low = jnp.bfloat16
    scratch = []
    for chunk in chunks:
        full = chunk.shape(0)
        scratch += [pltpu.VMEM((2,) + full, low)] * 2
        scratch += [pltpu.VMEM(chunk.shape(k), low) for k in range(bits + 1)]
        scratch.append(pltpu.VMEM(full, low))
    stages = bits + 2
    per_chunk = 3 + 2 * bits
    scratch += [
        pltpu.VMEM((stages + 1,) + gains.shape, jnp.float32),
        pltpu.VMEM((stages,) + gains.shape, jnp.float32),
        pltpu.SemaphoreType.DMA((len(chunks) * per_chunk,)),
        pltpu.SemaphoreType.DMA((len(chunks) * per_chunk,)),
        pltpu.SemaphoreType.DMA((len(chunks) * 2,)),
        pltpu.SemaphoreType.DMA((stages,)),
        pltpu.SemaphoreType.DMA((stages,)),
        pltpu.SemaphoreType.DMA((len(chunks),)),
    ]
    anywhere = pl.BlockSpec(memory_space=pl.ANY)
    in_vmem = pl.BlockSpec(memory_space=pltpu.VMEM)
    return pl.pallas_call(
        functools.partial(reduce_kernel, chunks, bits),
        out_shape=tuple(
            jax.ShapeDtypeStruct((a.shape[0] // ways, a.shape[1]), low) for a in (attn, ffn, down)
        )
        + (jax.ShapeDtypeStruct(gains.shape, jnp.float32),),
        in_specs=[anywhere] * 3 + [in_vmem],
        out_specs=(anywhere,) * 3 + (in_vmem,),
        scratch_shapes=scratch,
        compiler_params=pltpu.CompilerParams(
            collective_id=0, has_side_effects=True, vmem_limit_bytes=56 * 2**20
        ),
        name="reduce_grads",
    )(attn, ffn, down, gains)


def gather_kernel(plan, *refs):
    count = len({item[0] for item in plan})
    shards, outs = refs[:count], refs[count : 2 * count]
    send_sem, recv_sem, local_sem = refs[2 * count :]
    rep, fsdp = lax.axis_index("rep"), lax.axis_index("fsdp")
    core, far = lax.rem(fsdp, 2), lax.div(fsdp, 2)
    half = lax.rem(rep, 2)
    other = (1 - far) * 2 + core
    sibling = (rep, far * 2 + 1 - core)
    across = (rep, other)
    twin = (rep + 1 - 2 * half, fsdp)

    barrier = pltpu.get_barrier_semaphore()
    for peer in (sibling, across, twin):
        pl.semaphore_signal(barrier, inc=1, device_id=peer, device_id_type=MESH)
    pl.semaphore_wait(barrier, 3)

    waiting = []

    def send(c, slot, src, dst, peer):
        copy = pltpu.make_async_remote_copy(
            src_ref=src,
            dst_ref=dst,
            send_sem=send_sem.at[c * 5 + slot],
            recv_sem=recv_sem.at[c * 5 + slot],
            device_id=peer,
            device_id_type=MESH,
        )
        copy.start()
        waiting.append(copy)
        return copy

    def run_chunk(c, item):
        which, dim, start, size = item
        shard, out = shards[which], outs[which]
        height = shard.shape[0]

        def view(ref, owner, part):
            begin, extent = start, size
            if part is not None:
                extent = size // 2
                begin = start + part * extent
            if dim == 0:
                first = begin if owner is None else owner * height + begin
                return ref.at[pl.ds(pl.multiple_of(first, 16), extent), :]
            first = 0 if owner is None else pl.multiple_of(owner * height, 16)
            return ref.at[pl.ds(first, height), pl.ds(pl.multiple_of(begin, 128), extent)]

        over = send(
            c, 0, view(shard, None, half), view(out, fsdp, half), across
        )
        near = [send(c, 1, view(shard, None, None), view(out, fsdp, None), sibling)]
        keep = pltpu.make_async_copy(
            view(shard, None, None), view(out, fsdp, None), local_sem.at[c]
        )
        keep.start()
        yield
        over.wait_recv()
        got = view(out, other, half)
        swap = send(c, 2, got, got, twin)
        near.append(send(c, 3, got, got, sibling))
        yield
        swap.wait_recv()
        rest = view(out, other, 1 - half)
        near.append(send(c, 4, rest, rest, sibling))
        yield
        for copy in near:
            copy.wait_recv()
        keep.wait()

    todo = [run_chunk(c, item) for c, item in enumerate(plan)]
    run_staggered(todo, GATHER_AHEAD)
    for copy in waiting:
        copy.wait_send()


def gather_weights(arrays):
    ways = lax.axis_size("fsdp")
    plan = []
    for i, array in enumerate(arrays):
        if array.shape[1] % 256 == 0:
            parts = [(i, 1, a, b) for a, b in cut(array.shape[1], 256, GATHER_MOST)]
        else:
            step = array.shape[0] // 2
            parts = [(i, 0, 0, step), (i, 0, step, step)]
        plan += parts
    anywhere = pl.BlockSpec(memory_space=pl.ANY)
    return pl.pallas_call(
        functools.partial(gather_kernel, plan),
        out_shape=tuple(
            jax.ShapeDtypeStruct((a.shape[0] * ways, a.shape[1]), a.dtype) for a in arrays
        ),
        in_specs=[pl.BlockSpec(memory_space=pltpu.VMEM)] * len(arrays),
        out_specs=(anywhere,) * len(arrays),
        scratch_shapes=[
            pltpu.SemaphoreType.DMA((len(plan) * 5,)),
            pltpu.SemaphoreType.DMA((len(plan) * 5,)),
            pltpu.SemaphoreType.DMA((len(plan),)),
        ],
        compiler_params=pltpu.CompilerParams(
            collective_id=1, has_side_effects=True, vmem_limit_bytes=32 * 2**20
        ),
        name="gather_weights",
    )(*arrays)


def body(
    tokens,
    cotangent,
    lengths,
    norm1_gain,
    w_query,
    w_key,
    w_value,
    w_out,
    norm2_gain,
    w_gate,
    w_up,
    w_down,
):
    gains = jnp.stack([norm1_gain, norm2_gain])
    gains = jnp.pad(gains, ((0, 14), (0, -gains.shape[1] % 256)))
    attn_shard = jnp.concatenate([w_query, w_key, w_value, w_out], axis=1)
    attn_weight, gate_weight, up_weight, down_weight, all_gains = gather_weights(
        [attn_shard, w_gate, w_up, w_down, gains]
    )
    width = w_query.shape[0]
    all_gains = all_gains.reshape(-1, 16, all_gains.shape[1])[:, :2, :width]
    gain_one, gain_two = all_gains[:, 0].reshape(-1), all_gains[:, 1].reshape(-1)
    splits = [w_query.shape[1], w_key.shape[1], w_value.shape[1]]
    key_at, value_at, out_at = splits[0], sum(splits[:2]), sum(splits)
    qkv_weight = attn_weight[:, :out_at]
    out_weight = attn_weight[:, out_at:]
    count = tokens.shape[0]
    ways = lax.axis_size("fsdp")
    total = count * ways
    head_dim = HEAD_DIM
    scale = head_dim ** (-0.5)
    segment_all, position_all = doc_layout(lengths[0], total)
    first_row = lax.axis_index("fsdp") * count
    segment_mine = lax.dynamic_slice_in_dim(segment_all, first_row, count)
    position_mine = lax.dynamic_slice_in_dim(position_all, first_row, count)
    place_mine = first_row + jnp.arange(count, dtype=jnp.int32)
    inputs = tokens.astype(jnp.float32)
    inverse_one = lax.rsqrt(jnp.mean(inputs * inputs, axis=-1, keepdims=True) + EPS)
    gain_one_f = gain_one.astype(jnp.float32)
    normed_one = (inputs * inverse_one * gain_one_f).astype(jnp.bfloat16)
    qkv = matmul(normed_one, qkv_weight)
    query = rotate(
        qkv[:, :key_at].reshape(count, -1, head_dim), position_mine, 1.0
    ).astype(jnp.bfloat16)
    key_local = rotate(
        qkv[:, key_at:value_at].reshape(count, -1, head_dim), position_mine, 1.0
    ).astype(jnp.bfloat16)
    value_local = qkv[:, value_at:].astype(jnp.bfloat16)
    all_keys, all_values = (
        lax.all_gather(key_local.reshape(count, -1), "fsdp", axis=0, tiled=True),
        lax.all_gather(value_local, "fsdp", axis=0, tiled=True),
    )
    groups = all_keys.shape[1] // head_dim
    share = query.shape[1] // groups
    grouped = query.reshape(count, groups, share, head_dim)
    key_block = min(512, total)
    nblocks = total // key_block
    key_blocks = all_keys.reshape(nblocks, key_block, groups, head_dim)
    value_blocks = all_values.reshape(nblocks, key_block, groups, head_dim)
    segment_blocks = segment_all.reshape(nblocks, key_block)
    place_blocks = jnp.arange(total, dtype=jnp.int32).reshape(nblocks, key_block)

    def scores_for(keys_here, segment_here, place_here):
        allowed = (place_here[None, :] <= place_mine[:, None]) & (
            segment_here[None, :] == segment_mine[:, None]
        )
        raw = (
            jnp.einsum("bgrd,kgd->grbk", grouped, keys_here, preferred_element_type=jnp.float32)
            * scale
        )
        return (jnp.where(allowed[None, None], raw, -1e30), allowed[None, None])

    def gather_stats(carry, item):
        top, mass = carry
        keys_here, values_here, segment_here, place_here = item
        raw, allowed = scores_for(keys_here, segment_here, place_here)
        new_top = jnp.maximum(top, jnp.max(raw, axis=-1, keepdims=True))
        expo = jnp.where(allowed, jnp.exp(raw - new_top), 0.0)
        mass = mass * jnp.exp(top - new_top) + jnp.sum(expo, axis=-1, keepdims=True)
        return ((new_top, mass), None)

    stack = (key_blocks, value_blocks, segment_blocks, place_blocks)
    start_top = jnp.full((groups, share, count, 1), -1e30, jnp.float32)
    start_mass = jnp.zeros((groups, share, count, 1), jnp.float32)
    (top_all, mass_all), unused = lax.scan(gather_stats, (start_top, start_mass), stack)
    log_total = top_all + jnp.log(mass_all)

    def probs_for(item):
        keys_here, values_here, segment_here, place_here = item
        raw, allowed = scores_for(keys_here, segment_here, place_here)
        return jnp.where(allowed, jnp.exp(raw - log_total), 0.0)

    def mix_values(carry, item):
        probs = probs_for(item).astype(jnp.bfloat16)
        return (
            carry
            + jnp.einsum("grbk,kgd->bgrd", probs, item[1], preferred_element_type=jnp.float32),
            None,
        )

    attended, unused = lax.scan(
        mix_values, jnp.zeros((count, groups, share, head_dim), jnp.float32), stack
    )
    attended_flat = attended.reshape(count, -1)
    attended_low = attended_flat.astype(jnp.bfloat16)
    resid = inputs + matmul(attended_low, out_weight)
    inverse_two = lax.rsqrt(jnp.mean(resid * resid, axis=-1, keepdims=True) + EPS)
    gain_two_f = gain_two.astype(jnp.float32)
    normed_two = (resid * inverse_two * gain_two_f).astype(jnp.bfloat16)
    gate = matmul(normed_two, gate_weight)
    up_proj = matmul(normed_two, up_weight)
    sigma = jax.nn.sigmoid(gate)
    activated = gate * sigma
    hidden = (activated * up_proj).astype(jnp.bfloat16)
    mixed = (resid + matmul(hidden, down_weight)).astype(jnp.bfloat16)
    upstream = cotangent.astype(jnp.float32)
    down_grad = left_inner(hidden, cotangent)
    hidden_back = right_inner(cotangent, down_weight)
    gate_back = (hidden_back * up_proj * sigma * (1.0 + gate * (1.0 - sigma))).astype(jnp.bfloat16)
    up_back = (hidden_back * activated).astype(jnp.bfloat16)
    ffn_grad = left_inner(normed_two, jnp.concatenate([gate_back, up_back], axis=1))
    normed_two_back = right_inner(gate_back, gate_weight) + right_inner(up_back, up_weight)
    norm2_grad, resid_part = norm_back(resid, inverse_two, gain_two_f, normed_two_back)
    resid_back = upstream + resid_part
    branch_back = resid_back.astype(jnp.bfloat16)
    out_grad = left_inner(attended_low, branch_back)
    attended_back = right_inner(branch_back, out_weight).astype(jnp.bfloat16)
    back_heads = attended_back.reshape(count, groups, share, head_dim)
    delta = jnp.sum(back_heads.astype(jnp.float32) * attended, axis=-1).transpose(1, 2, 0)[
        ..., None
    ]

    def attend_back(carry, item):
        probs = probs_for(item)
        keys_here = item[0]
        values_here = item[1]
        values_back = jnp.einsum(
            "grbk,bgrd->kgd",
            probs.astype(jnp.bfloat16),
            back_heads,
            preferred_element_type=jnp.float32,
        )
        prob_back = jnp.einsum(
            "bgrd,kgd->grbk", back_heads, values_here, preferred_element_type=jnp.float32
        )
        score_back = (probs * (prob_back - delta)).astype(jnp.bfloat16)
        carry = carry + jnp.einsum(
            "grbk,kgd->bgrd", score_back, keys_here, preferred_element_type=jnp.float32
        )
        keys_back = (
            jnp.einsum("grbk,bgrd->kgd", score_back, grouped, preferred_element_type=jnp.float32)
            * scale
        )
        return (carry, (keys_back, values_back))

    query_acc, kv_back = lax.scan(
        attend_back, jnp.zeros((count, groups, share, head_dim), jnp.float32), stack
    )
    keys_back_all = kv_back[0].reshape(total, -1)
    values_back_all = kv_back[1].reshape(total, -1)
    keys_back, values_back = (
        lax.psum_scatter(
            keys_back_all.astype(jnp.bfloat16), "fsdp", scatter_dimension=0, tiled=True
        ).astype(jnp.float32),
        lax.psum_scatter(
            values_back_all.astype(jnp.bfloat16), "fsdp", scatter_dimension=0, tiled=True
        ).astype(jnp.float32),
    )
    key_pre = (
        rotate(keys_back.reshape(count, -1, head_dim), position_mine, -1.0)
        .reshape(count, -1)
        .astype(jnp.bfloat16)
    )
    value_pre = values_back.astype(jnp.bfloat16)
    query_pre = (
        rotate((query_acc * scale).reshape(count, -1, head_dim), position_mine, -1.0)
        .reshape(count, -1)
        .astype(jnp.bfloat16)
    )
    qkv_pre = jnp.concatenate([query_pre, key_pre, value_pre], axis=1)
    qkv_grad = left_inner(normed_one, qkv_pre)
    normed_one_back = right_inner(qkv_pre, qkv_weight)
    norm1_grad, input_part = norm_back(inputs, inverse_one, gain_one_f, normed_one_back)
    tokens_grad = (resid_back + input_part).astype(jnp.bfloat16)
    low = jnp.bfloat16
    attn_grad = jnp.concatenate([qkv_grad.astype(low), out_grad.astype(low)], axis=1)
    gains = jnp.stack([norm1_grad, norm2_grad])
    gains = jnp.pad(gains, ((0, 6), (0, -gains.shape[1] % 128)))
    attn_sum, ffn_sum, down_sum, gain_sum = reduce_grads(
        attn_grad, ffn_grad.astype(low), down_grad.astype(low), gains
    )
    mine = lax.axis_index("fsdp") * norm1_gain.shape[0]
    gain_rows = lax.dynamic_slice_in_dim(gain_sum, mine, norm1_gain.shape[0], axis=1)
    results = []
    offset = 0
    for shard in (w_query, w_key, w_value, w_out):
        results.append(attn_sum[:, offset : offset + shard.shape[1]].astype(jnp.float32))
        offset += shard.shape[1]
    hidden_size = w_gate.shape[1]
    return (
        mixed,
        tokens_grad,
        gain_rows[0],
        results[0],
        results[1],
        results[2],
        results[3],
        gain_rows[1],
        ffn_sum[:, :hidden_size].astype(jnp.float32),
        ffn_sum[:, hidden_size:].astype(jnp.float32),
        down_sum.astype(jnp.float32),
    )


def solution(mesh):
    return jax.shard_map(
        body,
        mesh=mesh,
        in_specs=(
            P(("rep", "fsdp"), None),
            P(("rep", "fsdp"), None),
            P("rep", None),
            P("fsdp"),
            P("fsdp", None),
            P("fsdp", None),
            P("fsdp", None),
            P("fsdp", None),
            P("fsdp"),
            P("fsdp", None),
            P("fsdp", None),
            P("fsdp", None),
        ),
        out_specs=(
            P(("rep", "fsdp"), None),
            P(("rep", "fsdp"), None),
            P("fsdp"),
            P("fsdp", None),
            P("fsdp", None),
            P("fsdp", None),
            P("fsdp", None),
            P("fsdp"),
            P("fsdp", None),
            P("fsdp", None),
            P("fsdp", None),
        ),
        check_vma=False,
    )
```
